32 devices in a mesh: node: 4 (over x, core), seq: 8 (over z, y).
Axes of the slice: x: 2, y: 2, z: 4, core: 2. Of those that a mesh axis runs over, the one named last changes fastest.
Arguments:
- tokens: bfloat16 [4096, 2560], P(('node', 'seq')), may hold values from -6 to 6
- grad_out: bfloat16 [4096, 2560], P(('node', 'seq')), may hold values from -6 to 6
- expert_ids: int32 [4096, 6], P(('node', 'seq')), may hold values from 0 to 31, all different within a row; in each aligned block of 128 rows (0 to 127, 128 to 255, ...) at most 28 rows name the same one
- gate_weights: float32 [4096, 6], P(('node', 'seq')), may hold values from 0.1 to 1
- w_gate: bfloat16 [32, 2560, 768], P(('node', 'seq')), may hold values from -0.125 to 0.125
- w_up: bfloat16 [32, 2560, 768], P(('node', 'seq')), may hold values from -0.125 to 0.125
- w_down: bfloat16 [32, 768, 2560], P(('node', 'seq')), may hold values from -0.21875 to 0.21875
Outputs:
- grad_tokens: bfloat16 [4096, 2560], P(('node', 'seq'))
- grad_gate: bfloat16 [32, 2560, 768], P(('node', 'seq'))
- grad_up: bfloat16 [32, 2560, 768], P(('node', 'seq'))
- grad_down: bfloat16 [32, 768, 2560], P(('node', 'seq'))
The draws below stay inside these ranges and needn't reach their ends.
Inputs may be any that keep to these rules, and one draw needn't show every extreme that they name: `expert_ids`: among the rows of one device no expert is named more than 28 times, a bound that some block reaches; the 6 experts of a token differ.
All inputs are finite; a program needn't handle non-finite values.
Results may differ from the reference program's by a relative error of at most 0.0064.
Values may be sent and summed in bfloat16 or wider, within the bound.
A program may use at most 128 MiB of HBM per device.

```python
import math
import jax
import jax.numpy as jnp
import numpy as np
from jax import lax

D = 2560
FE = 768
TOP = 6
TOK_DEV = 128
EXPERTS = 32
TOKENS = 4096
CAP = 28
DEVICES = 32


def levels(rng, dims, cuts, smallest, high):
    gain, own = 1.0, jax.random.fold_in(rng, 6)
    for axis_at, blocks in cuts:
        draws = jnp.exp(jax.random.uniform(jax.random.fold_in(own, axis_at), (blocks,), jnp.float32, smallest / len(cuts), high / len(cuts)))
        gain = gain * jnp.repeat(draws, dims[axis_at] // blocks).reshape([-1 if axis == axis_at else 1 for axis in range(len(dims))])
    return gain


def deal_out(own_key, own, number, rows, count, top, bound, skew):
    sequence = jax.random.permutation(own_key, count)
    heavy_load, ordinary = portions_of(count, rows * top, bound, skew, True), portions_of(count, rows * top, bound, skew, False)
    places = jnp.arange(count)

    def named(sizes, rotation):
        used = int((sizes > 0).sum())
        fixed = max(1, used // 4)
        moved = fixed + (places - fixed + rotation * (used - fixed)) % max(1, count - fixed)
        return jnp.zeros((count,), jnp.int32).at[sequence[jnp.where(places < fixed, places, moved)]].set(jnp.asarray(sizes, jnp.int32))

    sizes = jnp.where(number % 4 == 0, named(heavy_load, number // 4), named(ordinary, number - number // 4 - 1))
    mixed = jax.random.permutation(jax.random.fold_in(own, 3), count)
    giver, taker = mixed[0:count // 2 * 2:2], mixed[1:count // 2 * 2:2]
    room = jnp.minimum(sizes[giver] - 1, bound - sizes[taker]) // 2
    room = jnp.where((giver == sequence[0]) | (taker == sequence[0]) | (sizes[taker] == 0), 0, jnp.maximum(room, 0))
    moved = jax.random.randint(jax.random.fold_in(own, 4), (count // 2,), 0, 1 << 20) % (room + 1)
    sizes = sizes.at[giver].add(-moved).at[taker].add(moved)
    labels = jnp.searchsorted(jnp.cumsum(sizes), jnp.arange(rows * top), side="right").astype(jnp.int32)
    table = labels.reshape(top, rows).T
    table = table[jax.random.permutation(jax.random.fold_in(own, 1), rows)]
    rotation = jax.random.randint(jax.random.fold_in(own, 2), (rows, 1), 0, top)
    return jnp.take_along_axis(table, (jnp.arange(top)[None, :] + rotation) % top, axis=1)


def portions_of(count, total, reach, slope, full):
    portions = [(1 << 20) // math.isqrt(grade ** slope) + 1 for grade in range(1, count + 1)]
    largest = reach if full else min(reach, max(-(-total // count), total * portions[0] // sum(portions)))
    least = 1 if total - largest >= count - 1 else 0
    counts, surplus = [largest] + [least] * (count - 1), total - largest - least * (count - 1)
    while surplus > 0:
        movable = [i for i in range(1, count) if counts[i] < largest] or [i for i in range(1, count) if counts[i] < reach]
        whole, left = sum([portions[i] for i in movable]), surplus
        for i in movable:
            extra = min(reach - counts[i], max(1, left * portions[i] // whole), surplus)
            counts[i] = counts[i] + extra
            surplus = surplus - extra
    return np.array(counts)


def noise(key, shape, scale, limit, split=(), kind=jnp.bfloat16):
    drawn = jax.random.normal(key, shape, jnp.float32) * scale
    if len(split) > 0:
        drawn = levels(key, shape, split, -0.22, 0.18) * drawn
    return jnp.clip(drawn, min=-limit, max=limit).astype(kind)


def setup_inputs(seed: int = 0) -> dict:
    key_list = jax.random.split(jax.random.key(seed), 8)
    tokens = noise(key_list[0], (TOKENS, D), 1.0, 6.0, ((0, 32),))
    grad_out = noise(key_list[1], (TOKENS, D), 1.0, 6.0, ((0, 32),))
    expert_ids_keys = jax.random.split(jax.random.fold_in(key_list[2], 1), TOKENS // TOK_DEV)
    expert_ids_turns = jax.random.permutation(jax.random.fold_in(key_list[2], 3), TOKENS // TOK_DEV)
    expert_ids = jax.vmap(lambda own, number: deal_out(jax.random.fold_in(key_list[2], 2), own, number, TOK_DEV, EXPERTS, TOP, CAP, 2))(expert_ids_keys, expert_ids_turns).reshape((TOKENS, TOP))
    gate_weights = jnp.clip(0.1 + 0.9 * jax.random.uniform(key_list[3], (TOKENS, TOP), jnp.float32) ** levels(key_list[3], (TOKENS, TOP), ((0, 32),), -0.2, 0.2), 0.1, 1.0)
    w_gate = noise(key_list[4], (EXPERTS, D, FE), D ** -0.5, 0.125, ((0, 32),))
    w_up = noise(key_list[5], (EXPERTS, D, FE), D ** -0.5, 0.125, ((0, 32),))
    w_down = noise(key_list[6], (EXPERTS, FE, D), FE ** -0.5, 0.21875, ((0, 32),))
    return dict(tokens=tokens, grad_out=grad_out, expert_ids=expert_ids, gate_weights=gate_weights, w_gate=w_gate, w_up=w_up, w_down=w_down)


def expert_backward(rows_in, rows_grad, weight_gate, weight_up, weight_down):
    gate_pre = jnp.dot(rows_in, weight_gate, preferred_element_type=jnp.float32)
    up_pre = jnp.dot(rows_in, weight_up, preferred_element_type=jnp.float32)
    sigmoid_gate = jax.nn.sigmoid(gate_pre)
    activation = (gate_pre * sigmoid_gate * up_pre).astype(jnp.bfloat16)
    act_grad = jnp.dot(rows_grad, weight_down.T, preferred_element_type=jnp.float32)
    gate_grad = (act_grad * up_pre * sigmoid_gate * (1.0 + gate_pre * (1.0 - sigmoid_gate))).astype(jnp.bfloat16)
    up_grad = (act_grad * gate_pre * sigmoid_gate).astype(jnp.bfloat16)
    down_wgrad = jnp.dot(activation.T, rows_grad, preferred_element_type=jnp.float32).astype(jnp.bfloat16)
    gate_wgrad = jnp.dot(rows_in.T, gate_grad, preferred_element_type=jnp.float32).astype(jnp.bfloat16)
    up_wgrad = jnp.dot(rows_in.T, up_grad, preferred_element_type=jnp.float32).astype(jnp.bfloat16)
    input_grad = (jnp.dot(gate_grad, weight_gate.T, preferred_element_type=jnp.float32)
                  + jnp.dot(up_grad, weight_up.T, preferred_element_type=jnp.float32)).astype(jnp.bfloat16)
    return gate_wgrad, up_wgrad, down_wgrad, input_grad


def one_expert(operands):
    return expert_backward(*operands)


def reference(tokens, grad_out, expert_ids, gate_weights, w_gate, w_up, w_down):
    flat_ids = expert_ids.reshape(-1).astype(jnp.int32)
    entries = flat_ids.shape[0]
    per_block = TOK_DEV * TOP
    slot_count = DEVICES * CAP
    one_hot = (flat_ids.reshape(DEVICES, per_block, 1)
               == jnp.arange(EXPERTS, dtype=jnp.int32)[None, None, :]).astype(jnp.int32)
    slot_rank = (jnp.sum(jnp.cumsum(one_hot, axis=1) * one_hot, axis=2).reshape(-1) - 1).astype(jnp.int32)
    block_of = jnp.arange(entries, dtype=jnp.int32) // per_block
    slot_index = (flat_ids * slot_count + block_of * CAP + slot_rank).astype(jnp.int32)
    slot_source = jnp.full((EXPERTS * slot_count,), entries, jnp.int32).at[slot_index].set(
        jnp.arange(entries, dtype=jnp.int32))
    occupied = slot_source < entries
    clipped = jnp.minimum(slot_source, entries - 1)
    token_of = clipped // TOP
    slot_gate = jnp.where(occupied, gate_weights.reshape(-1)[clipped], jnp.zeros((), jnp.float32))
    rows_in = jnp.where(occupied[:, None], tokens[token_of], jnp.zeros((), jnp.bfloat16))
    rows_grad = (slot_gate[:, None] * grad_out[token_of].astype(jnp.float32)).astype(jnp.bfloat16)
    rows_in = rows_in.reshape(EXPERTS, slot_count, D)
    rows_grad = rows_grad.reshape(EXPERTS, slot_count, D)
    gate_wgrad, up_wgrad, down_wgrad, input_grad = lax.map(
        one_expert, (rows_in, rows_grad, w_gate, w_up, w_down))
    input_flat = input_grad.reshape(EXPERTS * slot_count, D)
    pair_grad = input_flat[slot_index].astype(jnp.float32).reshape(-1, TOP, D)
    grad_tokens = jnp.sum(pair_grad, axis=1).astype(jnp.bfloat16)
    return grad_tokens, gate_wgrad, up_wgrad, down_wgrad
```

```python
import functools

import jax
import jax.numpy as jnp
from jax import lax
from jax.experimental import pallas as pl
from jax.experimental.pallas import tpu as pltpu
from jax.sharding import PartitionSpec as P

BF = jnp.bfloat16
F32 = jnp.float32
MESH = pl.DeviceIdType.MESH


def dot(a, b, ca=1, cb=0):
    return lax.dot_general(a, b, (((ca,), (cb,)), ((), ())), preferred_element_type=F32)


def kernel(
    sizes,
    info, tokens, grad, wg, wu, wd,
    gt, wgo, wuo, wdo,
    xall, snd, rcv, mm, infog, scale, wgv, wuv, wdv, gp, up, ag, act, gg, ug, rrv, zrv,
    info_send, info_recv, ag_send, ag_recv, pl_send, pl_recv, rt_send, rt_recv, zr_send, zr_recv,
    x_sem, w_sem, o_sem,
):
    Z, inner, NP, S, cap, R, top, tok, C, W, FE = sizes
    T = Z * tok
    rows = NP * R
    half = rows // 2
    n = lax.axis_index("node")
    s = lax.axis_index("seq")
    z = s // inner
    y = lax.rem(s, inner)
    me = n * inner + y

    def plane_dev(p):
        return (p // inner, z * inner + lax.rem(p, inner))

    def line_dev(zz):
        return (n, zz * inner + y)

    def own(a, i):
        return xall.at[i, pl.ds(pl.multiple_of(a * tok, 16), tok)]

    loads = []
    for i in range(2 * C):
        src = (tokens if i < C else grad).at[:, (i % C) * W:(i % C + 1) * W]
        load = pltpu.make_async_copy(src, own(z, i), x_sem.at[i])
        load.start()
        loads.append(load)
    pltpu.make_async_copy(wg, wgv, w_sem.at[0]).start()
    pltpu.make_async_copy(wu, wuv, w_sem.at[1]).start()
    for c in range(C):
        pltpu.make_async_copy(wd.at[:, c * W:(c + 1) * W], wdv.at[c], w_sem.at[2]).start()
    infog[z] = info[...]

    barrier = pltpu.get_barrier_semaphore()

    @pl.loop(1, NP)
    def _(d):
        pl.semaphore_signal(barrier, inc=1, device_id=plane_dev(lax.rem(me + d, NP)), device_id_type=MESH)

    for d in range(1, Z):
        pl.semaphore_signal(barrier, inc=1, device_id=line_dev(lax.rem(z + d, Z)), device_id_type=MESH)
    pl.semaphore_wait(barrier, NP - 1 + Z - 1)

    def info_copy(d):
        return pltpu.make_async_remote_copy(
            infog.at[z], infog.at[z], info_send.at[d], info_recv.at[d],
            device_id=line_dev(lax.rem(z + d, Z)), device_id_type=MESH)

    for d in range(1, Z):
        info_copy(d).start()
    for load in loads:
        load.wait()

    def ag_copy(j, step, way):
        shard = z - step if way == 0 else z + step
        to = z + 1 if way == 0 else z - 1
        ref = own(shard, j)
        return pltpu.make_async_remote_copy(
            ref, ref, ag_send.at[j, step, way], ag_recv.at[j, step, way],
            device_id=line_dev(to), device_id_type=MESH)

    def ag_sends(step, way):
        if way == 0:
            return (z >= step) & (z < Z - 1)
        return (z <= Z - 1 - step) & (z > 0)

    def ag_arrives(step, way):
        if way == 0:
            return z - 1 >= step
        return z + 1 <= Z - 1 - step

    def ag_in(j, step, way):
        shard = z - 1 - step if way == 0 else z + 1 + step
        ref = own(shard, j)
        return pltpu.make_async_remote_copy(
            ref, ref, ag_send.at[j, step, way], ag_recv.at[j, step, way],
            device_id=line_dev(z), device_id_type=MESH)

    def peer_rows(p):
        return pl.ds(pl.multiple_of(p * R, 16), R)

    def plane_copy(src, dst, p, send, recv):
        return pltpu.make_async_remote_copy(
            src.at[peer_rows(p)], dst.at[peer_rows(me)], send, recv,
            device_id=plane_dev(p), device_id_type=MESH)

    def plane_start(src, dst, send, recv):
        @pl.loop(1, NP)
        def _(d):
            plane_copy(src, dst, lax.rem(me + d, NP), send, recv).start()

    def wait_bytes(ref, sem):
        pltpu.make_async_copy(ref, ref, sem).wait()

    others = pl.ds(0, (NP - 1) * R)

    def routing():
        for d in range(1, Z):
            info_copy(d).wait_send()
            pltpu.make_async_remote_copy(
                infog.at[z], infog.at[lax.rem(z - d + Z, Z)], info_send.at[d], info_recv.at[d],
                device_id=line_dev(z), device_id_type=MESH).wait_recv()
        p_of = lax.broadcasted_iota(jnp.int32, (NP, tok), 0)
        expert = ((p_of // inner) * S + z * inner + lax.rem(p_of, inner)).astype(F32)
        before = (lax.broadcasted_iota(jnp.int32, (tok, tok), 0)
                  < lax.broadcasted_iota(jnp.int32, (tok, tok), 1)).astype(F32).astype(BF)
        slots, gates = [], []
        for zz in range(Z):
            table = infog[zz]
            hit = jnp.zeros((NP, tok), F32)
            gate = jnp.zeros((NP, tok), F32)
            for k in range(top):
                same = table[k:k + 1, :] == expert
                hit = hit + same.astype(F32)
                gate = gate + jnp.where(same, table[8 + k:9 + k, :], 0.0)
            rank = dot(hit.astype(BF), before) + float(zz * cap)
            slots.append(jnp.where(hit > 0.0, rank, -1.0))
            gates.append(gate)
        slot = jnp.concatenate(slots, axis=1)
        gate = jnp.concatenate(gates, axis=1)
        slot_id = lax.broadcasted_iota(jnp.int32, (R, T), 0).astype(F32)
        for p in range(NP):
            pick = slot_id == slot[p:p + 1, :]
            mm[p * R:(p + 1) * R, :] = pick.astype(F32).astype(BF)
            scale[p * R:(p + 1) * R, :] = jnp.sum(
                jnp.where(pick, gate[p:p + 1, :], 0.0), axis=1, keepdims=True)

    def half_rows(h):
        return pl.ds(pl.multiple_of(h * half, 16), half)

    def gather(j):
        @pl.loop(0, 2)
        def _(h):
            picked = dot(mm[half_rows(h), :], xall[j])
            factor = jnp.where(j < C, 1.0, scale[half_rows(h), :])
            snd[j, half_rows(h), :] = (picked * factor).astype(BF)

        plane_start(snd.at[j], rcv.at[j], pl_send.at[j], pl_recv.at[j])
        rcv[j, peer_rows(me), :] = snd[j, peer_rows(me), :]

    def consume(k):
        wait_bytes(rcv.at[k, others], pl_recv.at[k])

        @pl.when(k == 0)
        def _():
            wait_bytes(wgv, w_sem.at[0])
            wait_bytes(wuv, w_sem.at[1])
            wait_bytes(wdv, w_sem.at[2])

        @pl.when(k < C)
        def _():
            @pl.loop(0, 2)
            def _(h):
                block = rcv[k, half_rows(h), :]
                gp[half_rows(h), :] += dot(block, wgv[k])
                up[half_rows(h), :] += dot(block, wuv[k])

        @pl.when(k == C - 1)
        def _():
            @pl.loop(0, rows // 32)
            def _(h):
                part = pl.ds(pl.multiple_of(h * 32, 32), 32)
                g, u = gp[part, :], up[part, :]
                sig = jax.nn.sigmoid(g)
                act[part, :] = (g * sig * u).astype(BF)
                gp[part, :] = u * sig * (1.0 + g * (1.0 - sig))
                up[part, :] = g * sig

        @pl.when(k >= C)
        def _():
            @pl.loop(0, 2)
            def _(h):
                ag[half_rows(h), :] += dot(rcv[k, half_rows(h), :], wdv[k - C], 1, 1)

    @pl.loop(0, 2 * C + Z)
    def _(i):
        for step in range(Z):
            j = i - step

            @pl.when((j >= 0) & (j < 2 * C))
            def _():
                for way in range(2):
                    if step > 0:
                        @pl.when(ag_arrives(step - 1, way))
                        def _():
                            ag_in(j, step - 1, way).wait_recv()
                    if step < Z - 1:
                        @pl.when(ag_sends(step, way))
                        def _():
                            ag_copy(j, step, way).start()

        @pl.when(i == 0)
        def _():
            gp[...] = jnp.zeros_like(gp)
            up[...] = jnp.zeros_like(up)
            ag[...] = jnp.zeros_like(ag)
            routing()

        @pl.when((i >= Z - 1) & (i < 2 * C + Z - 1))
        def _():
            gather(i - (Z - 1))

        @pl.when(i >= Z)
        def _():
            consume(i - Z)

    @pl.loop(0, rows // 32)
    def _(h):
        part = pl.ds(pl.multiple_of(h * 32, 32), 32)
        gg[part, :] = (ag[part, :] * gp[part, :]).astype(BF)
        ug[part, :] = (ag[part, :] * up[part, :]).astype(BF)

    @pl.loop(0, 2 * C)
    def _(j):
        wait_bytes(snd.at[j, others], pl_send.at[j])
        for step in range(Z - 1):
            for way in range(2):
                @pl.when(ag_sends(step, way))
                def _():
                    ag_copy(j, step, way).wait_send()

    @pl.loop(0, C)
    def _(c):
        @pl.loop(0, 2)
        def _(h):
            snd[c, half_rows(h), :] = (
                dot(gg[half_rows(h), :], wgv[c], 1, 1) + dot(ug[half_rows(h), :], wuv[c], 1, 1)
            ).astype(BF)

        plane_start(snd.at[c], rrv.at[c], rt_send.at[c], rt_recv.at[c])
        rrv[c, peer_rows(me), :] = snd[c, peer_rows(me), :]

    def line_copy(c, d):
        to = lax.rem(z + d, Z)
        return pltpu.make_async_remote_copy(
            own(to, c), zrv.at[c, d - 1], zr_send.at[c, d], zr_recv.at[c, d],
            device_id=line_dev(to), device_id_type=MESH)

    def finish(c):
        total = xall[c, pl.ds(pl.multiple_of(z * tok, 16), tok), :].astype(F32)
        for d in range(1, Z):
            line_copy(c, d).wait_recv()
            total = total + zrv[c, d - 1].astype(F32)
        gt[c] = total.astype(BF)

    @pl.loop(0, C + 1)
    def _(c):
        @pl.when(c < C)
        def _():
            wgv[c] = dot(rcv[c], gg[...], 0, 0).astype(BF)
            pltpu.make_async_copy(wgv.at[c], wgo.at[c], o_sem.at[0, c]).start()
            wuv[c] = dot(rcv[c], ug[...], 0, 0).astype(BF)
            pltpu.make_async_copy(wuv.at[c], wuo.at[c], o_sem.at[1, c]).start()
            wdv[c] = dot(act[...], rcv[c + C], 0, 0).astype(BF)
            wait_bytes(rrv.at[c, others], rt_recv.at[c])
            xall[c] = dot(mm[...], rrv[c], 0, 0).astype(BF)
            for d in range(1, Z):
                line_copy(c, d).start()

        @pl.when(c > 0)
        def _():
            finish(c - 1)

    for c in range(C):
        pltpu.make_async_copy(wdv.at[c], wdo.at[:, c * W:(c + 1) * W], o_sem.at[2, c]).start()

    @pl.loop(0, C)
    def _(c):
        wait_bytes(snd.at[c, others], rt_send.at[c])
        for d in range(1, Z):
            line_copy(c, d).wait_send()
        wait_bytes(wgv.at[c], o_sem.at[0, c])
        wait_bytes(wuv.at[c], o_sem.at[1, c])
        wait_bytes(wdv.at[c], o_sem.at[2, c])


def local(tokens, grad_out, expert_ids, gate_weights, w_gate, w_up, w_down):
    tok, width = tokens.shape
    top = expert_ids.shape[1]
    N = lax.axis_size("node")
    S = lax.axis_size("seq")
    experts = N * S
    cap = max(2, (7 * top * tok + 6 * experts - 1) // (6 * experts))
    FE = w_gate.shape[2]
    Z = 4 if S % 4 == 0 else S
    inner = S // Z
    NP = N * inner
    R = -(-Z * cap // 16) * 16
    W = 512 if width % 512 == 0 else width
    C = width // W
    rows = NP * R
    sizes = (Z, inner, NP, S, cap, R, top, tok, C, W, FE)
    info = jnp.concatenate([
        jnp.pad(expert_ids.T.astype(F32), ((0, 8 - top), (0, 0))),
        jnp.pad(gate_weights.T, ((0, 8 - top), (0, 0))),
    ])
    any_spec = pl.BlockSpec(memory_space=pl.ANY)
    vmem_spec = pl.BlockSpec(memory_space=pltpu.VMEM)
    dma = pltpu.SemaphoreType.DMA
    gt, wgo, wuo, wdo = pl.pallas_call(
        functools.partial(kernel, sizes),
        out_shape=(
            jax.ShapeDtypeStruct((C, tok, W), BF),
            jax.ShapeDtypeStruct((C, W, FE), BF),
            jax.ShapeDtypeStruct((C, W, FE), BF),
            jax.ShapeDtypeStruct((FE, width), BF),
        ),
        in_specs=[vmem_spec] + [any_spec] * 5,
        out_specs=(vmem_spec, any_spec, any_spec, any_spec),
        scratch_shapes=[
            pltpu.VMEM((2 * C, Z * tok, W), BF),
            pltpu.VMEM((2 * C, rows, W), BF),
            pltpu.VMEM((2 * C, rows, W), BF),
            pltpu.VMEM((rows, Z * tok), BF),
            pltpu.VMEM((Z, 16, tok), F32),
            pltpu.VMEM((rows, 1), F32),
            pltpu.VMEM((C, W, FE), BF),
            pltpu.VMEM((C, W, FE), BF),
            pltpu.VMEM((C, FE, W), BF),
            pltpu.VMEM((rows, FE), F32),
            pltpu.VMEM((rows, FE), F32),
            pltpu.VMEM((rows, FE), F32),
            pltpu.VMEM((rows, FE), BF),
            pltpu.VMEM((rows, FE), BF),
            pltpu.VMEM((rows, FE), BF),
            pltpu.VMEM((C, rows, W), BF),
            pltpu.VMEM((C, Z - 1, tok, W), BF),
            dma((Z,)), dma((Z,)),
            dma((2 * C, Z - 1, 2)), dma((2 * C, Z - 1, 2)),
            dma((2 * C,)), dma((2 * C,)),
            dma((C,)), dma((C,)),
            dma((C, Z)), dma((C, Z)),
            dma((2 * C,)), dma((3,)), dma((3, C)),
        ],
        compiler_params=pltpu.CompilerParams(
            collective_id=0, has_side_effects=True, vmem_limit_bytes=63 * 1024 * 1024),
        cost_estimate=pl.CostEstimate(
            flops=16 * rows * width * FE, bytes_accessed=12 * width * FE, transcendentals=rows * FE),
    )(
        info, tokens, grad_out,
        w_gate[0].reshape(C, W, FE), w_up[0].reshape(C, W, FE), w_down[0],
    )
    grad_tokens = jnp.transpose(gt, (1, 0, 2)).reshape(tok, width)
    return (
        grad_tokens,
        wgo.reshape(1, width, FE),
        wuo.reshape(1, width, FE),
        wdo[None],
    )


def solution(mesh):
    spec2 = P(("node", "seq"), None)
    spec3 = P(("node", "seq"), None, None)
    return jax.shard_map(
        local,
        mesh=mesh,
        in_specs=(spec2, spec2, spec2, spec2, spec3, spec3, spec3),
        out_specs=(spec2, spec3, spec3, spec3),
        check_vma=False,
    )
```

```python
import functools

import jax
import jax.numpy as jnp
from jax import lax
from jax.experimental import pallas as pl
from jax.experimental.pallas import tpu as pltpu
from jax.sharding import PartitionSpec as P

BF = jnp.bfloat16
F32 = jnp.float32
MESH = pl.DeviceIdType.MESH


def dot(a, b, ca=1, cb=0):
    return lax.dot_general(a, b, (((ca,), (cb,)), ((), ())), preferred_element_type=F32)


def kernel(
    sizes,
    info, tokens, grad, wg, wu, wd,
    gt, wgv, wuv, wdv,
    xall, snd, rcv, mm, infog, scale, gp, up, ag, act, gg, ug, rrv, zrv, rly,
    info_send, info_recv, ag_send, ag_recv, pl_send, pl_recv, rt_send, rt_recv, zr_send, zr_recv,
    ry_recv, x_sem, w_sem,
):
    Z, inner, NP, S, cap, R, top, tok, C, W, FE = sizes
    T = Z * tok
    rows = NP * R
    half = rows // 2
    n = lax.axis_index("node")
    s = lax.axis_index("seq")
    z = s // inner
    y = lax.rem(s, inner)
    me = n * inner + y

    def plane_dev(p):
        return (p // inner, z * inner + lax.rem(p, inner))

    def line_dev(zz):
        return (n, zz * inner + y)

    def cols(c):
        return pl.ds(pl.multiple_of(c * W, 128), W)

    def own(a, i):
        return xall.at[i, pl.ds(pl.multiple_of(a * tok, 16), tok)]

    loads = []
    for i in range(2 * C):
        src = (tokens if i < C else grad).at[:, (i % C) * W:(i % C + 1) * W]
        load = pltpu.make_async_copy(src, own(z, i), x_sem.at[i])
        load.start()
        loads.append(load)
    pltpu.make_async_copy(wg, wgv, w_sem.at[0]).start()
    pltpu.make_async_copy(wu, wuv, w_sem.at[1]).start()
    pltpu.make_async_copy(wd, wdv, w_sem.at[2]).start()
    infog[z] = info[...]

    barrier = pltpu.get_barrier_semaphore()

    @pl.loop(1, NP)
    def _(d):
        pl.semaphore_signal(barrier, inc=1, device_id=plane_dev(lax.rem(me + d, NP)), device_id_type=MESH)

    for d in range(1, Z):
        pl.semaphore_signal(barrier, inc=1, device_id=line_dev(lax.rem(z + d, Z)), device_id_type=MESH)
    pl.semaphore_wait(barrier, NP - 1 + Z - 1)

    def info_copy(d):
        return pltpu.make_async_remote_copy(
            infog.at[z], infog.at[z], info_send.at[d], info_recv.at[d],
            device_id=line_dev(lax.rem(z + d, Z)), device_id_type=MESH)

    for d in range(1, Z):
        info_copy(d).start()
    for load in loads:
        load.wait()

    def ag_copy(j, step, way):
        shard = z - step if way == 0 else z + step
        to = z + 1 if way == 0 else z - 1
        ref = own(shard, j)
        return pltpu.make_async_remote_copy(
            ref, ref, ag_send.at[j, step, way], ag_recv.at[j, step, way],
            device_id=line_dev(to), device_id_type=MESH)

    def ag_sends(step, way):
        if way == 0:
            return (z >= step) & (z < Z - 1)
        return (z <= Z - 1 - step) & (z > 0)

    def ag_arrives(step, way):
        if way == 0:
            return z - 1 >= step
        return z + 1 <= Z - 1 - step

    def ag_in(j, step, way):
        shard = z - 1 - step if way == 0 else z + 1 + step
        ref = own(shard, j)
        return pltpu.make_async_remote_copy(
            ref, ref, ag_send.at[j, step, way], ag_recv.at[j, step, way],
            device_id=line_dev(z), device_id_type=MESH)

    def peer_rows(p):
        return pl.ds(pl.multiple_of(p * R, 16), R)

    def plane_copy(src, dst, p, send, recv):
        return pltpu.make_async_remote_copy(
            src.at[peer_rows(p)], dst.at[peer_rows(me)], send, recv,
            device_id=plane_dev(p), device_id_type=MESH)

    def plane_start(src, dst, send, recv):
        @pl.loop(1, NP)
        def _(d):
            plane_copy(src, dst, lax.rem(me + d, NP), send, recv).start()

    def wait_bytes(ref, sem):
        pltpu.make_async_copy(ref, ref, sem).wait()

    others = pl.ds(0, (NP - 1) * R)

    def routing():
        for d in range(1, Z):
            info_copy(d).wait_send()
            pltpu.make_async_remote_copy(
                infog.at[z], infog.at[lax.rem(z - d + Z, Z)], info_send.at[d], info_recv.at[d],
                device_id=line_dev(z), device_id_type=MESH).wait_recv()
        p_of = lax.broadcasted_iota(jnp.int32, (NP, tok), 0)
        expert = ((p_of // inner) * S + z * inner + lax.rem(p_of, inner)).astype(F32)
        before = (lax.broadcasted_iota(jnp.int32, (tok, tok), 0)
                  < lax.broadcasted_iota(jnp.int32, (tok, tok), 1)).astype(F32).astype(BF)
        slots, gates = [], []
        for zz in range(Z):
            table = infog[zz]
            hit = jnp.zeros((NP, tok), F32)
            gate = jnp.zeros((NP, tok), F32)
            for k in range(top):
                same = table[k:k + 1, :] == expert
                hit = hit + same.astype(F32)
                gate = gate + jnp.where(same, table[8 + k:9 + k, :], 0.0)
            rank = dot(hit.astype(BF), before) + float(zz * cap)
            slots.append(jnp.where(hit > 0.0, rank, -1.0))
            gates.append(gate)
        slot = jnp.concatenate(slots, axis=1)
        gate = jnp.concatenate(gates, axis=1)
        slot_id = lax.broadcasted_iota(jnp.int32, (R, T), 0).astype(F32)
        for p in range(NP):
            pick = slot_id == slot[p:p + 1, :]
            mm[p * R:(p + 1) * R, :] = pick.astype(F32).astype(BF)
            scale[p * R:(p + 1) * R, :] = jnp.sum(
                jnp.where(pick, gate[p:p + 1, :], 0.0), axis=1, keepdims=True)

    def half_rows(h):
        return pl.ds(pl.multiple_of(h * half, 16), half)

    def gather(j):
        @pl.loop(0, 2)
        def _(h):
            picked = dot(mm[half_rows(h), :], xall[j])
            factor = jnp.where(j < C, 1.0, scale[half_rows(h), :])
            snd[j, half_rows(h), :] = (picked * factor).astype(BF)

        plane_start(snd.at[j], rcv.at[j], pl_send.at[j], pl_recv.at[j])
        rcv[j, peer_rows(me), :] = snd[j, peer_rows(me), :]

    def consume(k):
        wait_bytes(rcv.at[k, others], pl_recv.at[k])

        @pl.when(k == 0)
        def _():
            wait_bytes(wgv, w_sem.at[0])
            wait_bytes(wuv, w_sem.at[1])
            wait_bytes(wdv, w_sem.at[2])

        @pl.when(k == 0)
        def _():
            @pl.loop(0, 2)
            def _(h):
                block = rcv[k, half_rows(h), :]
                gp[half_rows(h), :] = dot(block, wgv[k])
                up[half_rows(h), :] = dot(block, wuv[k])

        @pl.when((k > 0) & (k < C))
        def _():
            @pl.loop(0, 2)
            def _(h):
                block = rcv[k, half_rows(h), :]
                gp[half_rows(h), :] += dot(block, wgv[k])
                up[half_rows(h), :] += dot(block, wuv[k])

        @pl.when(k == C - 1)
        def _():
            @pl.loop(0, rows // 32)
            def _(h):
                part = pl.ds(pl.multiple_of(h * 32, 32), 32)
                g, u = gp[part, :], up[part, :]
                sig = jax.nn.sigmoid(g)
                act[part, :] = (g * sig * u).astype(BF)
                gp[part, :] = u * sig * (1.0 + g * (1.0 - sig))
                up[part, :] = g * sig

        @pl.when(k == C)
        def _():
            @pl.loop(0, 2)
            def _(h):
                ag[half_rows(h), :] = dot(rcv[k, half_rows(h), :], wdv[:, cols(k - C)], 1, 1)

        @pl.when(k > C)
        def _():
            @pl.loop(0, 2)
            def _(h):
                ag[half_rows(h), :] += dot(rcv[k, half_rows(h), :], wdv[:, cols(k - C)], 1, 1)

    @pl.loop(0, 2 * C + Z)
    def _(i):
        for step in range(Z):
            j = i - step

            @pl.when((j >= 0) & (j < 2 * C))
            def _():
                for way in range(2):
                    if step > 0:
                        @pl.when(ag_arrives(step - 1, way))
                        def _():
                            ag_in(j, step - 1, way).wait_recv()
                    if step < Z - 1:
                        @pl.when(ag_sends(step, way))
                        def _():
                            ag_copy(j, step, way).start()

        @pl.when(i == 0)
        def _():
            routing()

        @pl.when((i >= Z - 1) & (i < 2 * C + Z - 1))
        def _():
            gather(i - (Z - 1))

        @pl.when(i >= Z)
        def _():
            consume(i - Z)

    @pl.loop(0, rows // 32)
    def _(h):
        part = pl.ds(pl.multiple_of(h * 32, 32), 32)
        gg[part, :] = (ag[part, :] * gp[part, :]).astype(BF)
        ug[part, :] = (ag[part, :] * up[part, :]).astype(BF)

    @pl.loop(0, 2 * C)
    def _(j):
        wait_bytes(snd.at[j, others], pl_send.at[j])
        for step in range(Z - 1):
            for way in range(2):
                @pl.when(ag_sends(step, way))
                def _():
                    ag_copy(j, step, way).wait_send()

    @pl.loop(0, C)
    def _(c):
        @pl.loop(0, 2)
        def _(h):
            snd[c, half_rows(h), :] = (
                dot(gg[half_rows(h), :], wgv[c], 1, 1) + dot(ug[half_rows(h), :], wuv[c], 1, 1)
            ).astype(BF)

        plane_start(snd.at[c], rrv.at[c], rt_send.at[c], rt_recv.at[c])
        rrv[c, peer_rows(me), :] = snd[c, peer_rows(me), :]

    merge = Z == 4

    def line_copy(c, d):
        to = lax.rem(z + d, Z)
        return pltpu.make_async_remote_copy(
            own(to, c), zrv.at[c, d - 1], zr_send.at[c, d], zr_recv.at[c, d],
            device_id=line_dev(to), device_id_type=MESH)

    def relay_copy(c, d):
        return pltpu.make_async_remote_copy(
            own(lax.rem(z + d, Z), c), rly.at[c], zr_send.at[c, d], ry_recv.at[c],
            device_id=line_dev(z - 1 if d == 1 else z + 1), device_id_type=MESH)

    last = Z - 1
    middle = (z > 0) & (z < last)

    def send_partials(c):
        if merge:
            for d, end in ((1, last), (last, 0)):
                @pl.when(z == end)
                def _():
                    relay_copy(c, d).start()

            for d, end in ((1, last), (last, 0)):
                @pl.when(z != end)
                def _():
                    line_copy(c, d).start()

            @pl.when(~middle)
            def _():
                line_copy(c, 2).start()
        else:
            for d in range(1, Z):
                line_copy(c, d).start()

    def pass_on(c):
        if merge:
            @pl.when(middle)
            def _():
                relay_copy(c, 1).wait_recv()
                mine = pl.ds(pl.multiple_of(lax.rem(z + 2, Z) * tok, 16), tok)
                xall[c, mine, :] = (xall[c, mine, :].astype(F32) + rly[c].astype(F32)).astype(BF)
                line_copy(c, 2).start()

    def finish(c):
        total = xall[c, pl.ds(pl.multiple_of(z * tok, 16), tok), :].astype(F32)
        for d in range(1, Z):
            none = 0 if d == 1 else last
            if merge and d != 2:
                @pl.when(z != none)
                def _():
                    line_copy(c, d).wait_recv()

                total = total + jnp.where(z != none, zrv[c, d - 1].astype(F32), 0.0)
            else:
                line_copy(c, d).wait_recv()
                total = total + zrv[c, d - 1].astype(F32)
        gt[:, cols(c)] = total.astype(BF)

    @pl.loop(0, C + 2)
    def _(c):
        @pl.when(c < C)
        def _():
            wgv[c] = dot(rcv[c], gg[...], 0, 0).astype(BF)
            wuv[c] = dot(rcv[c], ug[...], 0, 0).astype(BF)
            wdv[:, cols(c)] = dot(act[...], rcv[c + C], 0, 0).astype(BF)
            wait_bytes(rrv.at[c, others], rt_recv.at[c])
            xall[c] = dot(mm[...], rrv[c], 0, 0).astype(BF)
            send_partials(c)

        @pl.when((c > 0) & (c < C + 1))
        def _():
            pass_on(c - 1)

        @pl.when(c > 1)
        def _():
            finish(c - 2)

    @pl.loop(0, C)
    def _(c):
        wait_bytes(snd.at[c, others], rt_send.at[c])
        for d in range(1, Z):
            line_copy(c, d).wait_send()


def local(tokens, grad_out, expert_ids, gate_weights, w_gate, w_up, w_down):
    tok, width = tokens.shape
    top = expert_ids.shape[1]
    N = lax.axis_size("node")
    S = lax.axis_size("seq")
    experts = N * S
    cap = max(2, (7 * top * tok + 6 * experts - 1) // (6 * experts))
    FE = w_gate.shape[2]
    Z = 4 if S % 4 == 0 else S
    inner = S // Z
    NP = N * inner
    R = -(-Z * cap // 16) * 16
    W = 256 if width % 256 == 0 else width
    C = width // W
    rows = NP * R
    sizes = (Z, inner, NP, S, cap, R, top, tok, C, W, FE)
    info = jnp.concatenate([
        jnp.pad(expert_ids.T.astype(F32), ((0, 8 - top), (0, 0))),
        jnp.pad(gate_weights.T, ((0, 8 - top), (0, 0))),
    ])
    any_spec = pl.BlockSpec(memory_space=pl.ANY)
    vmem_spec = pl.BlockSpec(memory_space=pltpu.VMEM)
    dma = pltpu.SemaphoreType.DMA
    gt, wgo, wuo, wdo = pl.pallas_call(
        functools.partial(kernel, sizes),
        out_shape=(
            pltpu.VMEM((tok, width), BF),
            pltpu.VMEM((C, W, FE), BF),
            pltpu.VMEM((C, W, FE), BF),
            pltpu.VMEM((FE, width), BF),
        ),
        in_specs=[vmem_spec] + [any_spec] * 5,
        out_specs=(vmem_spec,) * 4,
        scratch_shapes=[
            pltpu.VMEM((2 * C, Z * tok, W), BF),
            pltpu.VMEM((2 * C, rows, W), BF),
            pltpu.VMEM((2 * C, rows, W), BF),
            pltpu.VMEM((rows, Z * tok), BF),
            pltpu.VMEM((Z, 16, tok), F32),
            pltpu.VMEM((rows, 1), F32),
            pltpu.VMEM((rows, FE), F32),
            pltpu.VMEM((rows, FE), F32),
            pltpu.VMEM((rows, FE), F32),
            pltpu.VMEM((rows, FE), BF),
            pltpu.VMEM((rows, FE), BF),
            pltpu.VMEM((rows, FE), BF),
            pltpu.VMEM((C, rows, W), BF),
            pltpu.VMEM((C, Z - 1, tok, W), BF),
            pltpu.VMEM((C, tok, W), BF),
            dma((Z,)), dma((Z,)),
            dma((2 * C, Z - 1, 2)), dma((2 * C, Z - 1, 2)),
            dma((2 * C,)), dma((2 * C,)),
            dma((C,)), dma((C,)),
            dma((C, Z)), dma((C, Z)),
            dma((C,)), dma((2 * C,)), dma((3,)),
        ],
        compiler_params=pltpu.CompilerParams(
            collective_id=0, has_side_effects=True, vmem_limit_bytes=50 * 1024 * 1024),
        cost_estimate=pl.CostEstimate(
            flops=16 * rows * width * FE, bytes_accessed=12 * width * FE, transcendentals=rows * FE),
    )(
        info, tokens, grad_out,
        w_gate[0].reshape(C, W, FE), w_up[0].reshape(C, W, FE), w_down[0],
    )
    return (
        gt,
        wgo.reshape(1, width, FE),
        wuo.reshape(1, width, FE),
        wdo[None],
    )


def solution(mesh):
    spec2 = P(("node", "seq"), None)
    spec3 = P(("node", "seq"), None, None)
    return jax.shard_map(
        local,
        mesh=mesh,
        in_specs=(spec2, spec2, spec2, spec2, spec3, spec3, spec3),
        out_specs=(spec2, spec3, spec3, spec3),
        check_vma=False,
    )
```

```python
import functools

import jax
import jax.numpy as jnp
from jax import lax
from jax.experimental import pallas as pl
from jax.experimental.pallas import tpu as pltpu
from jax.sharding import PartitionSpec as P

BF = jnp.bfloat16
F32 = jnp.float32
MESH = pl.DeviceIdType.MESH


def dot(a, b, ca=1, cb=0):
    return lax.dot_general(a, b, (((ca,), (cb,)), ((), ())), preferred_element_type=F32)


def kernel(
    sizes,
    ids, gates, tokens, grad, wg, wu, wd,
    gt, wgv, wuv, wdv,
    xall, snd, rcv, mm, infog, scale, gp, up, ag, act, gg, ug, rrv, zrv, rly,
    info_send, info_recv, ag_send, ag_recv, pl_send, pl_recv, rt_send, rt_recv, zr_send, zr_recv,
    ry_recv, x_sem, w_sem,
):
    Z, inner, NP, S, cap, R, top, tok, C, W, FE = sizes
    T = Z * tok
    rows = NP * R
    half = rows // 2
    n = lax.axis_index("node")
    s = lax.axis_index("seq")
    z = s // inner
    y = lax.rem(s, inner)
    me = n * inner + y

    def plane_dev(p):
        return (p // inner, z * inner + lax.rem(p, inner))

    def line_dev(zz):
        return (n, zz * inner + y)

    def cols(c):
        return pl.ds(pl.multiple_of(c * W, 128), W)

    def own(a, i):
        return xall.at[i, pl.ds(pl.multiple_of(a * tok, 16), tok)]

    loads = []
    for i in range(2 * C):
        src = (tokens if i < C else grad).at[:, (i % C) * W:(i % C + 1) * W]
        load = pltpu.make_async_copy(src, own(z, i), x_sem.at[i])
        load.start()
        loads.append(load)
    infog[z, 0:top, :] = ids[...].astype(F32)
    infog[z, 8:8 + top, :] = gates[...]

    barrier = pltpu.get_barrier_semaphore()

    @pl.loop(1, NP)
    def _(d):
        pl.semaphore_signal(barrier, inc=1, device_id=plane_dev(lax.rem(me + d, NP)), device_id_type=MESH)

    for d in range(1, Z):
        pl.semaphore_signal(barrier, inc=1, device_id=line_dev(lax.rem(z + d, Z)), device_id_type=MESH)
    pl.semaphore_wait(barrier, NP - 1 + Z - 1)

    def info_copy(d):
        return pltpu.make_async_remote_copy(
            infog.at[z], infog.at[z], info_send.at[d], info_recv.at[d],
            device_id=line_dev(lax.rem(z + d, Z)), device_id_type=MESH)

    for d in range(1, Z):
        info_copy(d).start()
    for load in loads:
        load.wait()

    def ag_copy(j, step, way):
        shard = z - step if way == 0 else z + step
        to = z + 1 if way == 0 else z - 1
        ref = own(shard, j)
        return pltpu.make_async_remote_copy(
            ref, ref, ag_send.at[j, step, way], ag_recv.at[j, step, way],
            device_id=line_dev(to), device_id_type=MESH)

    def ag_sends(step, way):
        if way == 0:
            return (z >= step) & (z < Z - 1)
        return (z <= Z - 1 - step) & (z > 0)

    def ag_arrives(step, way):
        if way == 0:
            return z - 1 >= step
        return z + 1 <= Z - 1 - step

    def ag_in(j, step, way):
        shard = z - 1 - step if way == 0 else z + 1 + step
        ref = own(shard, j)
        return pltpu.make_async_remote_copy(
            ref, ref, ag_send.at[j, step, way], ag_recv.at[j, step, way],
            device_id=line_dev(z), device_id_type=MESH)

    def peer_rows(p):
        return pl.ds(pl.multiple_of(p * R, 16), R)

    def plane_copy(src, dst, p, send, recv):
        return pltpu.make_async_remote_copy(
            src.at[peer_rows(p)], dst.at[peer_rows(me)], send, recv,
            device_id=plane_dev(p), device_id_type=MESH)

    def plane_start(src, dst, send, recv):
        @pl.loop(1, NP)
        def _(d):
            plane_copy(src, dst, lax.rem(me + d, NP), send, recv).start()

    def wait_bytes(ref, sem):
        pltpu.make_async_copy(ref, ref, sem).wait()

    others = pl.ds(0, (NP - 1) * R)

    def routing():
        for d in range(1, Z):
            info_copy(d).wait_send()
            pltpu.make_async_remote_copy(
                infog.at[z], infog.at[lax.rem(z - d + Z, Z)], info_send.at[d], info_recv.at[d],
                device_id=line_dev(z), device_id_type=MESH).wait_recv()
        p_of = lax.broadcasted_iota(jnp.int32, (NP, tok), 0)
        expert = ((p_of // inner) * S + z * inner + lax.rem(p_of, inner)).astype(F32)
        before = (lax.broadcasted_iota(jnp.int32, (tok, tok), 0)
                  < lax.broadcasted_iota(jnp.int32, (tok, tok), 1)).astype(F32).astype(BF)
        slots, gates = [], []
        for zz in range(Z):
            table = infog[zz]
            hit = jnp.zeros((NP, tok), F32)
            gate = jnp.zeros((NP, tok), F32)
            for k in range(top):
                same = table[k:k + 1, :] == expert
                hit = hit + same.astype(F32)
                gate = gate + jnp.where(same, table[8 + k:9 + k, :], 0.0)
            rank = dot(hit.astype(BF), before) + float(zz * cap)
            slots.append(jnp.where(hit > 0.0, rank, -1.0))
            gates.append(gate)
        slot = jnp.concatenate(slots, axis=1)
        gate = jnp.concatenate(gates, axis=1)
        slot_id = lax.broadcasted_iota(jnp.int32, (R, T), 0).astype(F32)
        for p in range(NP):
            pick = slot_id == slot[p:p + 1, :]
            mm[p * R:(p + 1) * R, :] = pick.astype(F32).astype(BF)
            scale[p * R:(p + 1) * R, :] = jnp.sum(
                jnp.where(pick, gate[p:p + 1, :], 0.0), axis=1, keepdims=True)

    def half_rows(h):
        return pl.ds(pl.multiple_of(h * half, 16), half)

    def gather(j):
        @pl.loop(0, 2)
        def _(h):
            picked = dot(mm[half_rows(h), :], xall[j])
            factor = jnp.where(j < C, 1.0, scale[half_rows(h), :])
            snd[j, half_rows(h), :] = (picked * factor).astype(BF)

        plane_start(snd.at[j], rcv.at[j], pl_send.at[j], pl_recv.at[j])
        rcv[j, peer_rows(me), :] = snd[j, peer_rows(me), :]

    def consume(k):
        wait_bytes(rcv.at[k, others], pl_recv.at[k])

        @pl.when(k == 0)
        def _():
            wait_bytes(wgv, w_sem.at[0])
            wait_bytes(wuv, w_sem.at[1])
            wait_bytes(wdv, w_sem.at[2])

        @pl.when(k == 0)
        def _():
            @pl.loop(0, 2)
            def _(h):
                block = rcv[k, half_rows(h), :]
                gp[half_rows(h), :] = dot(block, wgv[k])
                up[half_rows(h), :] = dot(block, wuv[k])

        @pl.when((k > 0) & (k < C))
        def _():
            @pl.loop(0, 2)
            def _(h):
                block = rcv[k, half_rows(h), :]
                gp[half_rows(h), :] += dot(block, wgv[k])
                up[half_rows(h), :] += dot(block, wuv[k])

        @pl.when(k == C - 1)
        def _():
            @pl.loop(0, rows // 32)
            def _(h):
                part = pl.ds(pl.multiple_of(h * 32, 32), 32)
                g, u = gp[part, :], up[part, :]
                sig = jax.nn.sigmoid(g)
                act[part, :] = (g * sig * u).astype(BF)
                gp[part, :] = u * sig * (1.0 + g * (1.0 - sig))
                up[part, :] = g * sig

        @pl.when(k == C)
        def _():
            @pl.loop(0, 2)
            def _(h):
                ag[half_rows(h), :] = dot(rcv[k, half_rows(h), :], wdv[:, cols(k - C)], 1, 1)

        @pl.when((k > C) & (k < 2 * C - 1))
        def _():
            @pl.loop(0, 2)
            def _(h):
                ag[half_rows(h), :] += dot(rcv[k, half_rows(h), :], wdv[:, cols(k - C)], 1, 1)

        @pl.when(k == 2 * C - 1)
        def _():
            @pl.loop(0, 2)
            def _(h):
                part = half_rows(h)
                grad_act = ag[part, :] + dot(rcv[k, part, :], wdv[:, cols(k - C)], 1, 1)
                gg[part, :] = (grad_act * gp[part, :]).astype(BF)
                ug[part, :] = (grad_act * up[part, :]).astype(BF)

    lag = 1 + Z

    @pl.loop(0, 2 * C + lag)
    def _(i):
        for step in range(Z):
            j = i - step

            @pl.when((j >= 0) & (j < 2 * C))
            def _():
                for way in range(2):
                    if step > 0:
                        @pl.when(ag_arrives(step - 1, way))
                        def _():
                            ag_in(j, step - 1, way).wait_recv()
                    if step < Z - 1:
                        @pl.when(ag_sends(step, way))
                        def _():
                            ag_copy(j, step, way).start()

        @pl.when(i == 0)
        def _():
            pltpu.make_async_copy(wg, wgv, w_sem.at[0]).start()
            pltpu.make_async_copy(wu, wuv, w_sem.at[1]).start()
            pltpu.make_async_copy(wd, wdv, w_sem.at[2]).start()
            routing()

        @pl.when((i >= Z - 1) & (i < 2 * C + Z - 1))
        def _():
            gather(i - (Z - 1))

        @pl.when(i >= lag)
        def _():
            consume(i - lag)

    def line_sent(j):
        for step in range(Z - 1):
            for way in range(2):
                @pl.when(ag_sends(step, way))
                def _():
                    ag_copy(j, step, way).wait_send()

    @pl.loop(0, C)
    def _(c):
        wait_bytes(snd.at[c, others], pl_send.at[c])

        @pl.loop(0, 2)
        def _(h):
            snd[c, half_rows(h), :] = (
                dot(gg[half_rows(h), :], wgv[c], 1, 1) + dot(ug[half_rows(h), :], wuv[c], 1, 1)
            ).astype(BF)

        plane_start(snd.at[c], rrv.at[c], rt_send.at[c], rt_recv.at[c])
        rrv[c, peer_rows(me), :] = snd[c, peer_rows(me), :]

    merge = Z == 4

    def line_copy(c, d):
        to = lax.rem(z + d, Z)
        return pltpu.make_async_remote_copy(
            own(to, c), zrv.at[c, d - 1], zr_send.at[c, d], zr_recv.at[c, d],
            device_id=line_dev(to), device_id_type=MESH)

    def relay_copy(c, d):
        return pltpu.make_async_remote_copy(
            own(lax.rem(z + d, Z), c), rly.at[c], zr_send.at[c, d], ry_recv.at[c],
            device_id=line_dev(z - 1 if d == 1 else z + 1), device_id_type=MESH)

    last = Z - 1
    middle = (z > 0) & (z < last)

    def send_partials(c):
        if merge:
            for d, end in ((1, last), (last, 0)):
                @pl.when(z == end)
                def _():
                    relay_copy(c, d).start()

            for d, end in ((1, last), (last, 0)):
                @pl.when(z != end)
                def _():
                    line_copy(c, d).start()

            @pl.when(~middle)
            def _():
                line_copy(c, 2).start()
        else:
            for d in range(1, Z):
                line_copy(c, d).start()

    def pass_on(c):
        if merge:
            @pl.when(middle)
            def _():
                relay_copy(c, 1).wait_recv()
                mine = pl.ds(pl.multiple_of(lax.rem(z + 2, Z) * tok, 16), tok)
                xall[c, mine, :] = (xall[c, mine, :].astype(F32) + rly[c].astype(F32)).astype(BF)
                line_copy(c, 2).start()

    def finish(c):
        total = xall[c, pl.ds(pl.multiple_of(z * tok, 16), tok), :].astype(F32)
        for d in range(1, Z):
            none = 0 if d == 1 else last
            if merge and d != 2:
                @pl.when(z != none)
                def _():
                    line_copy(c, d).wait_recv()

                total = total + jnp.where(z != none, zrv[c, d - 1].astype(F32), 0.0)
            else:
                line_copy(c, d).wait_recv()
                total = total + zrv[c, d - 1].astype(F32)
        gt[:, cols(c)] = total.astype(BF)

    @pl.loop(0, C + 2)
    def _(c):
        @pl.when(c < C)
        def _():
            wgv[c] = dot(rcv[c], gg[...], 0, 0).astype(BF)
            wuv[c] = dot(rcv[c], ug[...], 0, 0).astype(BF)
            wdv[:, cols(c)] = dot(act[...], rcv[c + C], 0, 0).astype(BF)
            line_sent(c)
            line_sent(c + C)
            wait_bytes(snd.at[c + C, others], pl_send.at[c + C])
            wait_bytes(rrv.at[c, others], rt_recv.at[c])
            xall[c] = dot(mm[...], rrv[c], 0, 0).astype(BF)
            send_partials(c)

        @pl.when((c > 0) & (c < C + 1))
        def _():
            pass_on(c - 1)

        @pl.when(c > 1)
        def _():
            finish(c - 2)
            wait_bytes(snd.at[c - 2, others], rt_send.at[c - 2])
            for d in range(1, Z):
                line_copy(c - 2, d).wait_send()


def local(tokens, grad_out, expert_ids, gate_weights, w_gate, w_up, w_down):
    tok, width = tokens.shape
    top = expert_ids.shape[1]
    N = lax.axis_size("node")
    S = lax.axis_size("seq")
    experts = N * S
    cap = max(2, (7 * top * tok + 6 * experts - 1) // (6 * experts))
    FE = w_gate.shape[2]
    Z = 4 if S % 4 == 0 else S
    inner = S // Z
    NP = N * inner
    R = -(-Z * cap // 16) * 16
    W = 256 if width % 256 == 0 else width
    C = width // W
    rows = NP * R
    sizes = (Z, inner, NP, S, cap, R, top, tok, C, W, FE)
    any_spec = pl.BlockSpec(memory_space=pl.ANY)
    vmem_spec = pl.BlockSpec(memory_space=pltpu.VMEM)
    dma = pltpu.SemaphoreType.DMA
    gt, wgo, wuo, wdo = pl.pallas_call(
        functools.partial(kernel, sizes),
        out_shape=(
            pltpu.VMEM((tok, width), BF),
            pltpu.VMEM((C, W, FE), BF),
            pltpu.VMEM((C, W, FE), BF),
            pltpu.VMEM((FE, width), BF),
        ),
        in_specs=[vmem_spec] * 2 + [any_spec] * 5,
        out_specs=(vmem_spec,) * 4,
        scratch_shapes=[
            pltpu.VMEM((2 * C, Z * tok, W), BF),
            pltpu.VMEM((2 * C, rows, W), BF),
            pltpu.VMEM((2 * C, rows, W), BF),
            pltpu.VMEM((rows, Z * tok), BF),
            pltpu.VMEM((Z, 16, tok), F32),
            pltpu.VMEM((rows, 1), F32),
            pltpu.VMEM((rows, FE), F32),
            pltpu.VMEM((rows, FE), F32),
            pltpu.VMEM((rows, FE), F32),
            pltpu.VMEM((rows, FE), BF),
            pltpu.VMEM((rows, FE), BF),
            pltpu.VMEM((rows, FE), BF),
            pltpu.VMEM((C, rows, W), BF),
            pltpu.VMEM((C, Z - 1, tok, W), BF),
            pltpu.VMEM((C, tok, W), BF),
            dma((Z,)), dma((Z,)),
            dma((2 * C, Z - 1, 2)), dma((2 * C, Z - 1, 2)),
            dma((2 * C,)), dma((2 * C,)),
            dma((C,)), dma((C,)),
            dma((C, Z)), dma((C, Z)),
            dma((C,)), dma((2 * C,)), dma((3,)),
        ],
        compiler_params=pltpu.CompilerParams(
            collective_id=0, has_side_effects=True, vmem_limit_bytes=50 * 1024 * 1024),
        cost_estimate=pl.CostEstimate(
            flops=16 * rows * width * FE, bytes_accessed=12 * width * FE, transcendentals=rows * FE),
    )(
        expert_ids.T, gate_weights.T, tokens, grad_out,
        w_gate[0].reshape(C, W, FE), w_up[0].reshape(C, W, FE), w_down[0],
    )
    return (
        gt,
        wgo.reshape(1, width, FE),
        wuo.reshape(1, width, FE),
        wdo[None],
    )


def solution(mesh):
    spec2 = P(("node", "seq"), None)
    spec3 = P(("node", "seq"), None, None)
    return jax.shard_map(
        local,
        mesh=mesh,
        in_specs=(spec2, spec2, spec2, spec2, spec3, spec3, spec3),
        out_specs=(spec2, spec3, spec3, spec3),
        check_vma=False,
    )
```
